1024 devices in a mesh: expert: 64 (over z, core), dp: 16 (over x, y).
Axes of the slice: x: 4, y: 4, z: 32, core: 2. Of those that a mesh axis runs over, the one named last changes fastest.
Arguments:
- tokens: bfloat16 [8192, 2048], P('expert', 'dp'), may hold values from -6 to 6
- expert_ids: int32 [8192, 8], P('expert'), may hold values from 0 to 63, all different within a row; in each aligned block of 128 rows (0 to 127, 128 to 255, ...) at most 32 rows name the same one
- gate_weight: bfloat16 [64, 2048, 384], P('expert', 'dp'), may hold values from -0.125 to 0.125
- up_weight: bfloat16 [64, 2048, 384], P('expert', 'dp'), may hold values from -0.125 to 0.125
- hidden_grad: bfloat16 [64, 2048, 384], P('expert', 'dp'), may hold values from -6 to 6
Outputs:
- hidden: bfloat16 [64, 2048, 384], P('expert', 'dp')
- gate_grad: float32 [64, 2048, 384], P('expert', 'dp')
- up_grad: float32 [64, 2048, 384], P('expert', 'dp')
- token_grad: bfloat16 [8192, 2048], P('expert', 'dp')
The draws below stay inside these ranges and needn't reach their ends.
Inputs may be any that keep to these rules, and one draw needn't show every extreme that they name: `expert_ids`: each row names 8 different experts; among the 128 rows of one source no expert is named by more than 32 rows, a bound that some block reaches.
All inputs are finite; a program needn't handle non-finite values.
Results may differ from the reference program's by a relative error of at most 0.015.
Values may be sent and summed in bfloat16 or wider, within the bound.
No kernel may reach another device: no remote copies, remote signals or barrier semaphores. Data moves between devices by JAX's collectives and lax.ppermute only.
A program may use at most 32 MiB of HBM per device.

```python
import math
import jax
import jax.numpy as jnp
import numpy as np
from jax import lax

D = 2048
F = 384
TOK_DEV = 128
TOP = 8
EXPERTS = 64
CAP = 32
SLOTS = 2048
TOKENS = 8192
N_EXPERT = 64
N_DP = 16


def block_levels(own_key, extent, split, least, top_value):
    def one(position, parts):
        heights = jax.random.uniform(jax.random.fold_in(jax.random.fold_in(own_key, 6), position), (parts,), jnp.float32, least / len(split), top_value / len(split))
        return jnp.repeat(jnp.exp(heights), extent[position] // parts).reshape((-1,) + (1,) * (len(extent) - position - 1))

    loudness = one(*split[0])
    for cut in split[1:]:
        loudness = loudness * one(*cut)
    return loudness


def routed_block(key, own, number, rows, number_of, top, reach, slope):
    order = jax.random.permutation(key, number_of)
    crowded, common = shares(number_of, rows * top, reach, slope, True), shares(number_of, rows * top, reach, slope, False)
    places = jnp.arange(number_of)

    def named(lengths, offset_by):
        used = int((lengths > 0).sum())
        fixed = max(1, used // 4)
        moved = fixed + (places - fixed + offset_by * (used - fixed)) % max(1, number_of - fixed)
        return jnp.zeros((number_of,), jnp.int32).at[order[jnp.where(places < fixed, places, moved)]].set(jnp.asarray(lengths, jnp.int32))

    lengths = jnp.where(number % 4 == 0, named(crowded, number // 4), named(common, number - number // 4 - 1))
    mixed = jax.random.permutation(jax.random.fold_in(own, 3), number_of)
    giver, sink = mixed[0:number_of // 2 * 2:2], mixed[1:number_of // 2 * 2:2]
    slack = jnp.minimum(lengths[giver] - 1, reach - lengths[sink]) // 2
    slack = jnp.where((giver == order[0]) | (sink == order[0]) | (lengths[sink] == 0), 0, jnp.maximum(slack, 0))
    moved = jax.random.randint(jax.random.fold_in(own, 4), (number_of // 2,), 0, 1 << 20) % (slack + 1)
    lengths = lengths.at[giver].add(-moved).at[sink].add(moved)
    labels = jnp.searchsorted(jnp.cumsum(lengths), jnp.arange(rows * top), side="right").astype(jnp.int32)
    grid = labels.reshape(top, rows).T
    grid = grid[jax.random.permutation(jax.random.fold_in(own, 1), rows)]
    offset_by = jax.random.randint(jax.random.fold_in(own, 2), (rows, 1), 0, top)
    return jnp.take_along_axis(grid, (jnp.arange(top)[None, :] + offset_by) % top, axis=1)


def shares(count, total, limit, slope, full):
    portions = [(1 << 20) // math.isqrt(rank ** slope) + 1 for rank in range(1, count + 1)]
    largest = limit if full else min(limit, max(-(-total // count), total * portions[0] // sum(portions)))
    least = 1 if total - largest >= count - 1 else 0
    counts, rest = [largest] + [least] * (count - 1), total - largest - least * (count - 1)
    while rest > 0:
        movable = [i for i in range(1, count) if counts[i] < largest] or [i for i in range(1, count) if counts[i] < limit]
        whole, left = sum([portions[i] for i in movable]), rest
        for i in movable:
            addition = min(limit - counts[i], max(1, left * portions[i] // whole), rest)
            counts[i] = counts[i] + addition
            rest = rest - addition
    return np.array(counts)


def normal_values(own_key, shape, width, limit, shards=(), kind=jnp.bfloat16):
    gain = block_levels(own_key, shape, shards, -0.22, 0.18) if shards else 1.0
    values = jax.random.normal(own_key, shape, jnp.float32) * width * gain
    return jnp.minimum(jnp.maximum(values, -limit), limit).astype(kind)


def setup_inputs(seed: int = 0) -> dict:
    key_of = jax.random.split(jax.random.key(seed), 6)
    tokens = normal_values(key_of[0], (TOKENS, D), 1.0, 6.0, ((0, 64), (1, 16)))
    expert_ids_keys = jax.random.split(jax.random.fold_in(key_of[1], 1), TOKENS // TOK_DEV)
    expert_ids_turns = jax.random.permutation(jax.random.fold_in(key_of[1], 3), TOKENS // TOK_DEV)
    expert_ids = jax.vmap(lambda own, number: routed_block(jax.random.fold_in(key_of[1], 2), own, number, TOK_DEV, EXPERTS, TOP, CAP, 2))(expert_ids_keys, expert_ids_turns).reshape((TOKENS, TOP))
    gate_weight = normal_values(key_of[2], (EXPERTS, D, F), D ** -0.5, 0.125, ((0, 64), (1, 16)))
    up_weight = normal_values(key_of[3], (EXPERTS, D, F), D ** -0.5, 0.125, ((0, 64), (1, 16)))
    hidden_grad = normal_values(key_of[4], (EXPERTS, SLOTS, F), 1.0, 6.0, ((0, 64), (1, 16)))
    return {"tokens": tokens, "expert_ids": expert_ids, "gate_weight": gate_weight, "up_weight": up_weight, "hidden_grad": hidden_grad}


def reference(tokens, expert_ids, gate_weight, up_weight, hidden_grad):
    n_src = N_EXPERT
    n_dp = N_DP
    share = SLOTS // n_dp
    x_all = tokens.reshape(n_src, TOK_DEV, D).astype(jnp.float32)
    ids = expert_ids.reshape(n_src, TOK_DEV * TOP)
    ranks_cap = jnp.arange(CAP, dtype=jnp.int32)

    def per_expert(carry, expert):
        hit = (ids == expert).astype(jnp.int32)
        rank = jnp.cumsum(hit, axis=1) - hit
        pick = hit[..., None] * (rank[..., None] == ranks_cap).astype(jnp.int32)
        pick = pick.reshape(n_src, TOK_DEV, TOP, CAP).sum(2).astype(jnp.float32)
        rows = jnp.einsum('sir,sif->srf', pick, x_all).astype(jnp.bfloat16)
        rows_f = rows.reshape(n_dp, share, D).astype(jnp.float32)
        w_gate = lax.dynamic_index_in_dim(gate_weight, expert, 0, False).astype(jnp.float32)
        w_up = lax.dynamic_index_in_dim(up_weight, expert, 0, False).astype(jnp.float32)
        gate = jnp.einsum('dsk,kf->dsf', rows_f, w_gate)
        up = jnp.einsum('dsk,kf->dsf', rows_f, w_up)
        sig = jax.nn.sigmoid(gate)
        silu_gate = gate * sig
        hidden = (silu_gate * up).astype(jnp.bfloat16)
        delta = lax.dynamic_index_in_dim(hidden_grad, expert, 0, False).reshape(n_dp, share, F).astype(jnp.float32)
        gate_delta = (delta * up * sig * (1.0 + gate * (1.0 - sig))).astype(jnp.bfloat16).astype(jnp.float32)
        up_delta = (delta * silu_gate).astype(jnp.bfloat16).astype(jnp.float32)
        part_gate = lax.optimization_barrier(jnp.einsum('dsk,dsf->dkf', rows_f, gate_delta).astype(jnp.bfloat16))
        part_up = lax.optimization_barrier(jnp.einsum('dsk,dsf->dkf', rows_f, up_delta).astype(jnp.bfloat16))
        gate_sum = jnp.sum(part_gate.astype(jnp.float32), axis=0)
        up_sum = jnp.sum(part_up.astype(jnp.float32), axis=0)
        slot_grad = (jnp.einsum('dsf,kf->dsk', gate_delta, w_gate) + jnp.einsum('dsf,kf->dsk', up_delta, w_up)).astype(jnp.bfloat16)
        back = slot_grad.reshape(n_src, CAP, D).astype(jnp.float32)
        carry = carry + jnp.einsum('sir,srf->sif', pick, back)
        return carry, (hidden.reshape(SLOTS, F), gate_sum, up_sum)

    start = jnp.zeros((n_src, TOK_DEV, D), jnp.float32)
    total, outs = lax.scan(per_expert, start, jnp.arange(EXPERTS, dtype=jnp.int32))
    hidden, gate_grad, up_grad = outs
    token_grad = total.reshape(TOKENS, D).astype(jnp.bfloat16)
    return hidden, gate_grad, up_grad, token_grad
```

```python
import jax
import jax.numpy as jnp
from jax import lax
from jax.sharding import Mesh, PartitionSpec as P

CORES = 2


def on_device(tokens, expert_ids, gate_weight, up_weight, hidden_grad):
    n_z = lax.axis_size("z")
    n_dp = lax.axis_size("dp")
    core = lax.axis_index("c")
    swap = [(0, 1), (1, 0)]
    tok_rows, width_part = tokens.shape
    top_k = expert_ids.shape[1]
    share_rows = hidden_grad.shape[1]
    hidden_units = gate_weight.shape[2]
    capacity = share_rows * n_dp // (n_z * CORES)
    pair_rows = CORES * capacity

    own_rows = jnp.concatenate([gate_weight[0], up_weight[0]], axis=1)
    weights = lax.all_gather(own_rows, "dp", axis=0, tiled=True)

    other_tokens = lax.ppermute(tokens, "c", swap)
    other_ids = lax.ppermute(expert_ids, "c", swap)
    first = core == 0
    tokens_pair = jnp.concatenate(
        [jnp.where(first, tokens, other_tokens), jnp.where(first, other_tokens, tokens)], axis=0
    )
    ids_pair = jnp.concatenate(
        [jnp.where(first, expert_ids, other_ids), jnp.where(first, other_ids, expert_ids)], axis=0
    ).T
    pair_toks = CORES * tok_rows

    expert_of = jnp.arange(n_z, dtype=jnp.int32)[:, None] * CORES + core
    hit = jnp.zeros((n_z, pair_toks), jnp.bool_)
    for choice_k in range(top_k):
        hit = hit | (ids_pair[choice_k][None, :] == expert_of)
    src_of = jnp.arange(pair_toks, dtype=jnp.int32) // tok_rows
    earlier = (
        (jnp.arange(pair_toks)[:, None] < jnp.arange(pair_toks)[None, :])
        & (src_of[:, None] == src_of[None, :])
    ).astype(jnp.bfloat16)
    ranks = jnp.dot(hit.astype(jnp.bfloat16), earlier, preferred_element_type=jnp.float32)
    row_of = jnp.where(hit, ranks.astype(jnp.int32) + src_of[None, :] * capacity, -1)
    placer = (
        (row_of[:, None, :] == jnp.arange(pair_rows, dtype=jnp.int32)[None, :, None])
        .astype(jnp.bfloat16)
        .reshape(n_z * pair_rows, pair_toks)
    )
    outgoing = jnp.dot(placer, tokens_pair, preferred_element_type=jnp.float32)
    outgoing = outgoing.astype(jnp.bfloat16).reshape(n_z, pair_rows, width_part)
    own_width = lax.all_to_all(outgoing, "z", split_axis=0, concat_axis=0, tiled=True)
    by_share = own_width.reshape(n_dp, share_rows, width_part)
    arrived = lax.all_to_all(by_share, "dp", split_axis=0, concat_axis=0, tiled=True)
    slot_rows = arrived.transpose(1, 0, 2).reshape(share_rows, n_dp * width_part)

    both = jnp.dot(slot_rows, weights, preferred_element_type=jnp.float32)
    gate, up = both[:, :hidden_units], both[:, hidden_units:]
    sigmoid_gate = jax.nn.sigmoid(gate)
    silu_gate = gate * sigmoid_gate
    hidden = (silu_gate * up).astype(jnp.bfloat16)
    delta = hidden_grad[0].astype(jnp.float32)
    gate_delta = (delta * up * sigmoid_gate * (1.0 + gate * (1.0 - sigmoid_gate))).astype(
        jnp.bfloat16
    )
    up_delta = (delta * silu_gate).astype(jnp.bfloat16)
    both_delta = jnp.concatenate([gate_delta, up_delta], axis=1)
    all_delta = lax.all_gather(both_delta, "dp", axis=0, tiled=True)

    slot_grad = lax.dot_general(
        weights.reshape(n_dp, width_part, 2 * hidden_units),
        both_delta,
        (((2,), (1,)), ((), ())),
        preferred_element_type=jnp.float32,
    )
    slot_grad = slot_grad.astype(jnp.bfloat16).transpose(0, 2, 1)
    back = lax.all_to_all(slot_grad, "dp", split_axis=0, concat_axis=0, tiled=True)
    back = back.reshape(n_z, pair_rows, width_part)
    returned = lax.all_to_all(back, "z", split_axis=0, concat_axis=0, tiled=True)
    token_part = lax.dot_general(
        placer,
        returned.reshape(n_z * pair_rows, width_part),
        (((0,), (0,)), ((), ())),
        preferred_element_type=jnp.float32,
    )
    mine = jnp.where(first, token_part[:tok_rows], token_part[tok_rows:])
    theirs = jnp.where(first, token_part[tok_rows:], token_part[:tok_rows])
    token_grad = (mine + lax.ppermute(theirs, "c", swap)).astype(jnp.bfloat16)

    both_grad = lax.dot_general(
        own_width.reshape(n_dp * share_rows, width_part),
        all_delta,
        (((0,), (0,)), ((), ())),
        preferred_element_type=jnp.float32,
    )
    return (
        hidden[None],
        both_grad[None, :, :hidden_units],
        both_grad[None, :, hidden_units:],
        token_grad,
    )


def solution(mesh):
    n_expert, n_dp = mesh.devices.shape
    split = Mesh(mesh.devices.reshape(n_expert // CORES, CORES, n_dp), ("z", "c", "dp"))
    expert = ("z", "c")
    placed = (
        P(expert, "dp"),
        P(expert, None),
        P(expert, "dp", None),
        P(expert, "dp", None),
        P(expert, "dp", None),
    )
    return jax.shard_map(
        on_device,
        mesh=split,
        in_specs=placed,
        out_specs=(
            P(expert, "dp", None),
            P(expert, "dp", None),
            P(expert, "dp", None),
            P(expert, "dp"),
        ),
        check_vma=False,
    )
```

```python
import jax
import jax.numpy as jnp
from jax import lax
from jax.sharding import Mesh, PartitionSpec as P

CORES = 2
ZL = 4


def on_device(tokens, expert_ids, gate_weight, up_weight, hidden_grad):
    n_zh = lax.axis_size("zh")
    n_dp = lax.axis_size("dp")
    core = lax.axis_index("c")
    swap = [(0, 1), (1, 0)]
    tok_rows, width_part = tokens.shape
    top_k = expert_ids.shape[1]
    share_rows = hidden_grad.shape[1]
    hidden_units = gate_weight.shape[2]
    capacity = share_rows * n_dp // (n_zh * ZL * CORES)
    pair_rows = CORES * capacity

    own_rows = jnp.concatenate([gate_weight[0], up_weight[0]], axis=1)
    weights = lax.all_gather(own_rows, "dp", axis=0, tiled=True)

    ids_rows = expert_ids.T.astype(jnp.bfloat16)
    sent = jnp.concatenate([tokens, ids_rows], axis=0)
    mine = lax.all_gather(sent, "zh", axis=0, tiled=False)
    other = lax.ppermute(mine, "c", swap)
    first = core == 0
    known = jnp.stack([jnp.where(first, mine, other), jnp.where(first, other, mine)], axis=1)
    known_tokens = known[:, :, :tok_rows].reshape(n_zh, CORES * tok_rows, width_part)
    known_ids = known[:, :, tok_rows:].astype(jnp.float32)

    expert_of = (lax.axis_index("zh") * ZL + jnp.arange(ZL, dtype=jnp.int32)) * CORES + core
    expert_of = expert_of.astype(jnp.float32)[:, None, None, None]
    hit = jnp.zeros((ZL, n_zh, CORES, tok_rows), jnp.bool_)
    for choice_k in range(top_k):
        hit = hit | (known_ids[None, :, :, choice_k] == expert_of)
    earlier = jnp.arange(tok_rows)[:, None] < jnp.arange(tok_rows)[None, :]
    ranks = jnp.dot(
        hit.reshape(-1, tok_rows).astype(jnp.bfloat16),
        earlier.astype(jnp.bfloat16),
        preferred_element_type=jnp.float32,
    ).reshape(hit.shape)
    first_row = jnp.arange(CORES, dtype=jnp.int32)[None, None, :, None] * capacity
    row_of = jnp.where(hit, ranks.astype(jnp.int32) + first_row, -1)
    row_of = row_of.transpose(1, 0, 2, 3).reshape(n_zh, ZL, 1, CORES * tok_rows)
    placer = (
        (row_of == jnp.arange(pair_rows, dtype=jnp.int32)[:, None])
        .astype(jnp.bfloat16)
        .reshape(n_zh, ZL * pair_rows, CORES * tok_rows)
    )
    outgoing = lax.dot_general(
        placer, known_tokens, (((2,), (1,)), ((0,), (0,))), preferred_element_type=jnp.float32
    ).astype(jnp.bfloat16)
    outgoing = outgoing.reshape(n_zh, ZL, pair_rows, width_part).transpose(1, 0, 2, 3)
    own_width = lax.all_to_all(outgoing, "zl", split_axis=0, concat_axis=0, tiled=True)
    own_width = own_width.transpose(1, 0, 2, 3)
    by_share = own_width.reshape(n_dp, share_rows, width_part)
    arrived = lax.all_to_all(by_share, "dp", split_axis=0, concat_axis=0, tiled=True)
    slot_rows = arrived.transpose(1, 0, 2).reshape(share_rows, n_dp * width_part)

    both = jnp.dot(slot_rows, weights, preferred_element_type=jnp.float32)
    gate, up = both[:, :hidden_units], both[:, hidden_units:]
    sigmoid_gate = jax.nn.sigmoid(gate)
    silu_gate = gate * sigmoid_gate
    hidden = (silu_gate * up).astype(jnp.bfloat16)
    delta = hidden_grad[0].astype(jnp.float32)
    gate_delta = (delta * up * sigmoid_gate * (1.0 + gate * (1.0 - sigmoid_gate))).astype(
        jnp.bfloat16
    )
    up_delta = (delta * silu_gate).astype(jnp.bfloat16)
    both_delta = jnp.concatenate([gate_delta, up_delta], axis=1)
    all_delta = lax.all_gather(both_delta, "dp", axis=0, tiled=True)

    slot_grad = lax.dot_general(
        weights.reshape(n_dp, width_part, 2 * hidden_units),
        both_delta,
        (((2,), (1,)), ((), ())),
        preferred_element_type=jnp.float32,
    )
    slot_grad = slot_grad.astype(jnp.bfloat16).transpose(0, 2, 1)
    back = lax.all_to_all(slot_grad, "dp", split_axis=0, concat_axis=0, tiled=True)
    back = back.reshape(n_zh, ZL, pair_rows, width_part).transpose(1, 0, 2, 3)
    returned = lax.all_to_all(back, "zl", split_axis=0, concat_axis=0, tiled=True)
    returned = returned.transpose(1, 0, 2, 3).reshape(n_zh, ZL * pair_rows, width_part)
    token_part = lax.dot_general(
        placer, returned, (((1,), (1,)), ((0,), (0,))), preferred_element_type=jnp.float32
    ).reshape(n_zh, CORES, tok_rows, width_part)
    kept = jnp.where(first, token_part[:, 0], token_part[:, 1])
    given = jnp.where(first, token_part[:, 1], token_part[:, 0]).astype(jnp.bfloat16)
    token_sum = kept + lax.ppermute(given, "c", swap).astype(jnp.float32)
    token_grad = lax.psum_scatter(
        token_sum.astype(jnp.bfloat16), "zh", scatter_dimension=0, tiled=False
    )

    both_grad = lax.dot_general(
        own_width.reshape(n_dp * share_rows, width_part),
        all_delta,
        (((0,), (0,)), ((), ())),
        preferred_element_type=jnp.float32,
    )
    return (
        hidden[None],
        both_grad[None, :, :hidden_units],
        both_grad[None, :, hidden_units:],
        token_grad,
    )


def solution(mesh):
    n_expert, n_dp = mesh.devices.shape
    split = Mesh(mesh.devices.reshape(n_expert // (ZL * CORES), ZL, CORES, n_dp), ("zh", "zl", "c", "dp"))
    expert = ("zh", "zl", "c")
    placed = (
        P(expert, "dp"),
        P(expert, None),
        P(expert, "dp", None),
        P(expert, "dp", None),
        P(expert, "dp", None),
    )
    return jax.shard_map(
        on_device,
        mesh=split,
        in_specs=placed,
        out_specs=(
            P(expert, "dp", None),
            P(expert, "dp", None),
            P(expert, "dp", None),
            P(expert, "dp"),
        ),
        check_vma=False,
    )
```

```python
import jax
import jax.numpy as jnp
from jax import lax
from jax.sharding import Mesh, PartitionSpec as P

CORES = 2
ZL = 4


def gather_dp(rows, n_dp):
    copies = jnp.broadcast_to(rows[None], (n_dp, *rows.shape))
    got = lax.all_to_all(copies, "dp", split_axis=0, concat_axis=0, tiled=True)
    return got.reshape(n_dp * rows.shape[0], rows.shape[1])


def on_device(tokens, expert_ids, gate_weight, up_weight, hidden_grad):
    n_zh = lax.axis_size("zh")
    n_dp = lax.axis_size("dp")
    core = lax.axis_index("c")
    swap = [(0, 1), (1, 0)]
    tok_rows, width_part = tokens.shape
    top_k = expert_ids.shape[1]
    share_rows = hidden_grad.shape[1]
    hidden_units = gate_weight.shape[2]
    capacity = share_rows * n_dp // (n_zh * ZL * CORES)
    pair_rows = CORES * capacity

    own_rows = jnp.concatenate([gate_weight[0], up_weight[0]], axis=1)
    weights = gather_dp(own_rows, n_dp)

    ids_rows = expert_ids.T.astype(jnp.bfloat16)
    sent = jnp.concatenate([tokens, ids_rows], axis=0)
    mine = lax.all_gather(sent, "zh", axis=0, tiled=False)
    other = lax.ppermute(mine, "c", swap)
    first = core == 0
    known = jnp.stack([jnp.where(first, mine, other), jnp.where(first, other, mine)], axis=1)
    known_tokens = known[:, :, :tok_rows].reshape(n_zh, CORES * tok_rows, width_part)
    known_ids = known[:, :, tok_rows:].astype(jnp.float32)

    expert_of = (lax.axis_index("zh") * ZL + jnp.arange(ZL, dtype=jnp.int32)) * CORES + core
    expert_of = expert_of.astype(jnp.float32)[:, None, None, None]
    hit = jnp.zeros((ZL, n_zh, CORES, tok_rows), jnp.bool_)
    for choice_k in range(top_k):
        hit = hit | (known_ids[None, :, :, choice_k] == expert_of)
    earlier = jnp.arange(tok_rows)[:, None] < jnp.arange(tok_rows)[None, :]
    ranks = jnp.dot(
        hit.reshape(-1, tok_rows).astype(jnp.bfloat16),
        earlier.astype(jnp.bfloat16),
        preferred_element_type=jnp.float32,
    ).reshape(hit.shape)
    first_row = jnp.arange(CORES, dtype=jnp.int32)[None, None, :, None] * capacity
    row_of = jnp.where(hit, ranks.astype(jnp.int32) + first_row, -1)
    row_of = row_of.transpose(1, 0, 2, 3).reshape(n_zh, ZL, 1, CORES * tok_rows)
    placer = (
        (row_of == jnp.arange(pair_rows, dtype=jnp.int32)[:, None])
        .astype(jnp.bfloat16)
        .reshape(n_zh, ZL * pair_rows, CORES * tok_rows)
    )
    outgoing = lax.dot_general(
        placer, known_tokens, (((2,), (1,)), ((0,), (0,))), preferred_element_type=jnp.float32
    ).astype(jnp.bfloat16)
    outgoing = outgoing.reshape(n_zh, ZL, pair_rows, width_part).transpose(1, 0, 2, 3)
    outgoing, weights = lax.optimization_barrier((outgoing, weights))
    own_width = lax.all_to_all(outgoing, "zl", split_axis=0, concat_axis=0, tiled=True)
    own_width = own_width.transpose(1, 0, 2, 3)
    by_share = own_width.reshape(n_dp, share_rows, width_part)
    arrived = lax.all_to_all(by_share, "dp", split_axis=0, concat_axis=0, tiled=True)
    slot_rows = arrived.transpose(1, 0, 2).reshape(share_rows, n_dp * width_part)

    both = jnp.dot(slot_rows, weights, preferred_element_type=jnp.float32)
    gate, up = both[:, :hidden_units], both[:, hidden_units:]
    sigmoid_gate = jax.nn.sigmoid(gate)
    silu_gate = gate * sigmoid_gate
    hidden = (silu_gate * up).astype(jnp.bfloat16)
    delta = hidden_grad[0].astype(jnp.float32)
    gate_delta = (delta * up * sigmoid_gate * (1.0 + gate * (1.0 - sigmoid_gate))).astype(
        jnp.bfloat16
    )
    up_delta = (delta * silu_gate).astype(jnp.bfloat16)
    both_delta = jnp.concatenate([gate_delta, up_delta], axis=1)

    slot_grad = lax.dot_general(
        weights.reshape(n_dp, width_part, 2 * hidden_units),
        both_delta,
        (((2,), (1,)), ((), ())),
        preferred_element_type=jnp.float32,
    )
    slot_grad = slot_grad.astype(jnp.bfloat16).transpose(0, 2, 1)
    slot_grad, both_delta = lax.optimization_barrier((slot_grad, both_delta))
    all_delta = lax.all_gather(both_delta, "dp", axis=0, tiled=True)
    def go_back(slot_grad, placer):
        back = lax.all_to_all(slot_grad, "dp", split_axis=0, concat_axis=0, tiled=True)
        back = back.reshape(n_zh, ZL, pair_rows, width_part).transpose(1, 0, 2, 3)
        returned = lax.all_to_all(back, "zl", split_axis=0, concat_axis=0, tiled=True)
        returned = returned.transpose(1, 0, 2, 3).reshape(n_zh, ZL * pair_rows, width_part)
        token_part = lax.dot_general(
            placer, returned, (((1,), (1,)), ((0,), (0,))), preferred_element_type=jnp.float32
        ).reshape(n_zh, CORES, tok_rows, width_part)
        kept = jnp.where(first, token_part[:, 0], token_part[:, 1])
        given = jnp.where(first, token_part[:, 1], token_part[:, 0]).astype(jnp.bfloat16)
        token_sum = kept + lax.ppermute(given, "c", swap).astype(jnp.float32)
        sums = lax.all_to_all(
            token_sum.astype(jnp.bfloat16), "zh", split_axis=0, concat_axis=0, tiled=True
        )
        return jnp.sum(sums.astype(jnp.float32), axis=0).astype(jnp.bfloat16)

    token_grad = lax.cond(
        expert_ids[0, 0] >= 0, go_back, lambda *_: jnp.zeros_like(tokens), slot_grad, placer
    )

    both_grad = lax.dot_general(
        own_width.reshape(n_dp * share_rows, width_part),
        all_delta,
        (((0,), (0,)), ((), ())),
        preferred_element_type=jnp.float32,
    )
    return (
        hidden[None],
        both_grad[None, :, :hidden_units],
        both_grad[None, :, hidden_units:],
        token_grad,
    )


def solution(mesh):
    n_expert, n_dp = mesh.devices.shape
    split = Mesh(mesh.devices.reshape(n_expert // (ZL * CORES), ZL, CORES, n_dp), ("zh", "zl", "c", "dp"))
    expert = ("zh", "zl", "c")
    placed = (
        P(expert, "dp"),
        P(expert, None),
        P(expert, "dp", None),
        P(expert, "dp", None),
        P(expert, "dp", None),
    )
    return jax.shard_map(
        on_device,
        mesh=split,
        in_specs=placed,
        out_specs=(
            P(expert, "dp", None),
            P(expert, "dp", None),
            P(expert, "dp", None),
            P(expert, "dp"),
        ),
        check_vma=False,
    )
```

```python
import jax
import jax.numpy as jnp
from jax import lax
from jax.experimental import pallas as pl
from jax.experimental.pallas import tpu as pltpu
from jax.sharding import Mesh, PartitionSpec as P

CORES = 2
ZL = 4


def expert_kernel(rows_ref, weights_ref, grad_ref, hidden_ref, delta_ref, slot_grad_ref):
    n_dp, _, width_part = rows_ref.shape
    hidden_units = grad_ref.shape[1]
    rows = jnp.concatenate([rows_ref[part] for part in range(n_dp)], axis=1)
    both = jnp.dot(rows, weights_ref[...], preferred_element_type=jnp.float32)
    gate, up = both[:, :hidden_units], both[:, hidden_units:]
    sigmoid_gate = jax.nn.sigmoid(gate)
    silu_gate = gate * sigmoid_gate
    hidden_ref[...] = (silu_gate * up).astype(jnp.bfloat16)
    grad = grad_ref[...].astype(jnp.float32)
    delta_ref[:, :hidden_units] = (
        grad * up * sigmoid_gate * (1.0 + gate * (1.0 - sigmoid_gate))
    ).astype(jnp.bfloat16)
    delta_ref[:, hidden_units:] = (grad * silu_gate).astype(jnp.bfloat16)
    delta = delta_ref[...]
    for part in range(n_dp):
        slot_grad_ref[part] = lax.dot_general(
            delta,
            weights_ref[part * width_part : (part + 1) * width_part],
            (((1,), (1,)), ((), ())),
            preferred_element_type=jnp.float32,
        ).astype(jnp.bfloat16)


def experts(rows, weights, grad):
    n_dp, share_rows, width_part = rows.shape
    both_units = weights.shape[1]
    flops = 4 * share_rows * n_dp * width_part * both_units
    return pl.pallas_call(
        expert_kernel,
        out_shape=(
            jax.ShapeDtypeStruct((share_rows, both_units // 2), jnp.bfloat16),
            jax.ShapeDtypeStruct((share_rows, both_units), jnp.bfloat16),
            jax.ShapeDtypeStruct(rows.shape, jnp.bfloat16),
        ),
        compiler_params=pltpu.CompilerParams(vmem_limit_bytes=32 * 1024 * 1024),
        cost_estimate=pl.CostEstimate(
            flops=flops, bytes_accessed=2 * weights.size, transcendentals=grad.size
        ),
    )(rows, weights, grad)


def gather_dp(parts, n_dp):
    copies = [jnp.broadcast_to(part[None], (n_dp, *part.shape)) for part in parts]
    copies = jnp.concatenate(copies, axis=2) if len(parts) > 1 else copies[0]
    got = lax.all_to_all(copies, "dp", split_axis=0, concat_axis=0, tiled=True)
    return got.reshape(-1, got.shape[2])


def on_device(tokens, expert_ids, gate_weight, up_weight, hidden_grad):
    n_zh = lax.axis_size("zh")
    n_dp = lax.axis_size("dp")
    near = ("zl", "c")
    tok_rows, width_part = tokens.shape
    top_k = expert_ids.shape[1]
    share_rows = hidden_grad.shape[1]
    hidden_units = gate_weight.shape[2]
    capacity = share_rows * n_dp // (n_zh * ZL * CORES)

    weights = gather_dp([gate_weight[0], up_weight[0]], n_dp)

    ids_rows = expert_ids.T.astype(jnp.bfloat16)
    sent = jnp.concatenate([tokens, ids_rows], axis=0)
    known = lax.all_gather(sent, "zh", axis=0, tiled=False)
    known_tokens = known[:, :tok_rows]
    known_ids = known[:, tok_rows:].astype(jnp.float32)

    n_near = ZL * CORES
    expert_of = lax.axis_index("zh") * n_near + jnp.arange(n_near, dtype=jnp.int32)
    expert_of = expert_of.astype(jnp.float32)[None, :, None]
    hit = jnp.zeros((n_zh, n_near, tok_rows), jnp.bool_)
    for choice_k in range(top_k):
        hit = hit | (known_ids[:, choice_k][:, None] == expert_of)
    earlier = jnp.arange(tok_rows)[:, None] < jnp.arange(tok_rows)[None, :]
    ranks = jnp.dot(
        hit.reshape(-1, tok_rows).astype(jnp.bfloat16),
        earlier.astype(jnp.bfloat16),
        preferred_element_type=jnp.float32,
    ).reshape(hit.shape)
    row_of = jnp.where(hit, ranks.astype(jnp.int32), -1)[:, :, None]
    placer = (
        (row_of == jnp.arange(capacity, dtype=jnp.int32)[:, None])
        .astype(jnp.bfloat16)
        .reshape(n_zh, n_near * capacity, tok_rows)
    )
    outgoing = lax.dot_general(
        placer, known_tokens, (((2,), (1,)), ((0,), (0,))), preferred_element_type=jnp.float32
    ).astype(jnp.bfloat16)
    outgoing = outgoing.reshape(n_zh, n_near, capacity, width_part).transpose(1, 0, 2, 3)
    outgoing, weights = lax.optimization_barrier((outgoing, weights))
    own_width = lax.all_to_all(outgoing, near, split_axis=0, concat_axis=0, tiled=True)
    own_width = own_width.transpose(1, 0, 2, 3)
    by_share = own_width.reshape(n_dp, share_rows, width_part)
    arrived = lax.all_to_all(by_share, "dp", split_axis=0, concat_axis=0, tiled=True)
    hidden, both_delta, slot_grad = experts(arrived, weights, hidden_grad[0])
    all_delta = lax.all_gather(both_delta, "dp", axis=0, tiled=True)
    def go_back(slot_grad, placer):
        back = lax.all_to_all(slot_grad, "dp", split_axis=0, concat_axis=0, tiled=True)
        back = back.reshape(n_zh, n_near, capacity, width_part).transpose(1, 0, 2, 3)
        returned = lax.all_to_all(back, near, split_axis=0, concat_axis=0, tiled=True)
        returned = returned.transpose(1, 0, 2, 3).reshape(n_zh, n_near * capacity, width_part)
        token_sum = lax.dot_general(
            placer, returned, (((1,), (1,)), ((0,), (0,))), preferred_element_type=jnp.float32
        )
        sums = lax.all_to_all(
            token_sum.astype(jnp.bfloat16), "zh", split_axis=0, concat_axis=0, tiled=True
        )
        return jnp.sum(sums.astype(jnp.float32), axis=0).astype(jnp.bfloat16)

    token_grad = lax.cond(
        expert_ids[0, 0] >= 0, go_back, lambda *_: jnp.zeros_like(tokens), slot_grad, placer
    )

    both_grad = lax.dot_general(
        own_width.reshape(n_dp * share_rows, width_part),
        all_delta,
        (((0,), (0,)), ((), ())),
        preferred_element_type=jnp.float32,
    )
    return (
        hidden[None],
        both_grad[None, :, :hidden_units],
        both_grad[None, :, hidden_units:],
        token_grad,
    )


def solution(mesh):
    n_expert, n_dp = mesh.devices.shape
    split = Mesh(mesh.devices.reshape(n_expert // (ZL * CORES), ZL, CORES, n_dp), ("zh", "zl", "c", "dp"))
    expert = ("zh", "zl", "c")
    placed = (
        P(expert, "dp"),
        P(expert, None),
        P(expert, "dp", None),
        P(expert, "dp", None),
        P(expert, "dp", None),
    )
    return jax.shard_map(
        on_device,
        mesh=split,
        in_specs=placed,
        out_specs=(
            P(expert, "dp", None),
            P(expert, "dp", None),
            P(expert, "dp", None),
            P(expert, "dp"),
        ),
        check_vma=False,
    )
```

```python
import jax
import jax.numpy as jnp
from jax import lax
from jax.experimental import pallas as pl
from jax.experimental.pallas import tpu as pltpu
from jax.sharding import Mesh, PartitionSpec as P

CORES = 2
ZL = 4


def expert_kernel(rows_ref, gate_w_ref, up_w_ref, grad_ref, hidden_ref, delta_ref, slot_grad_ref):
    n_dp, _, width_part = rows_ref.shape
    hidden_units = grad_ref.shape[1]
    rows = jnp.concatenate([rows_ref[part] for part in range(n_dp)], axis=1)
    gate = jnp.dot(rows, gate_w_ref[...], preferred_element_type=jnp.float32)
    up = jnp.dot(rows, up_w_ref[...], preferred_element_type=jnp.float32)
    sigmoid_gate = jax.nn.sigmoid(gate)
    silu_gate = gate * sigmoid_gate
    hidden_ref[...] = (silu_gate * up).astype(jnp.bfloat16)
    grad = grad_ref[...].astype(jnp.float32)
    gate_delta = (grad * up * sigmoid_gate * (1.0 + gate * (1.0 - sigmoid_gate))).astype(
        jnp.bfloat16
    )
    up_delta = (grad * silu_gate).astype(jnp.bfloat16)
    delta_ref[:, :hidden_units] = gate_delta
    delta_ref[:, hidden_units:] = up_delta
    for part in range(n_dp):
        own = slice(part * width_part, (part + 1) * width_part)
        first = lax.dot_general(
            gate_delta,
            gate_w_ref[own],
            (((1,), (1,)), ((), ())),
            preferred_element_type=jnp.float32,
        )
        second = lax.dot_general(
            up_delta, up_w_ref[own], (((1,), (1,)), ((), ())), preferred_element_type=jnp.float32
        )
        slot_grad_ref[part] = (first + second).astype(jnp.bfloat16)


def experts(rows, gate_w, up_w, grad):
    share_rows, hidden_units = grad.shape
    return pl.pallas_call(
        expert_kernel,
        out_shape=(
            jax.ShapeDtypeStruct((share_rows, hidden_units), jnp.bfloat16),
            jax.ShapeDtypeStruct((share_rows, 2 * hidden_units), jnp.bfloat16),
            jax.ShapeDtypeStruct(rows.shape, jnp.bfloat16),
        ),
        compiler_params=pltpu.CompilerParams(vmem_limit_bytes=32 * 1024 * 1024),
        cost_estimate=pl.CostEstimate(
            flops=8 * share_rows * gate_w.size,
            bytes_accessed=4 * gate_w.size,
            transcendentals=grad.size,
        ),
    )(rows, gate_w, up_w, grad)


def weight_grad_kernel(rows_ref, delta_ref, gate_grad_ref, up_grad_ref):
    n_part, share_rows, _ = rows_ref.shape
    hidden_units = gate_grad_ref.shape[1]

    @pl.when(pl.program_id(0) == 0)
    def _():
        gate_grad_ref[...] = jnp.zeros_like(gate_grad_ref)
        up_grad_ref[...] = jnp.zeros_like(up_grad_ref)

    rows = rows_ref[...].reshape(n_part * share_rows, rows_ref.shape[2])
    both = lax.dot_general(
        rows, delta_ref[...], (((0,), (0,)), ((), ())), preferred_element_type=jnp.float32
    )
    gate_grad_ref[...] += both[:, :hidden_units]
    up_grad_ref[...] += both[:, hidden_units:]


def weight_grads(rows, delta):
    n_dp, share_rows, width_part = rows.shape
    both_units = delta.shape[1]
    step = n_dp // 4 if n_dp % 4 == 0 else n_dp
    out = jax.ShapeDtypeStruct((width_part, both_units // 2), jnp.float32)
    out_spec = pl.BlockSpec((width_part, both_units // 2), lambda i: (0, 0))
    return pl.pallas_call(
        weight_grad_kernel,
        grid=(n_dp // step,),
        in_specs=[
            pl.BlockSpec((step, share_rows, width_part), lambda i: (i, 0, 0)),
            pl.BlockSpec((step * share_rows, both_units), lambda i: (i, 0)),
        ],
        out_specs=(out_spec, out_spec),
        out_shape=(out, out),
        compiler_params=pltpu.CompilerParams(vmem_limit_bytes=32 * 1024 * 1024),
        cost_estimate=pl.CostEstimate(
            flops=2 * rows.size * both_units, bytes_accessed=2 * delta.size, transcendentals=0
        ),
    )(rows, delta)


def on_device(tokens, expert_ids, gate_weight, up_weight, hidden_grad):
    n_zh = lax.axis_size("zh")
    n_dp = lax.axis_size("dp")
    near = ("zl", "c")
    tok_rows, width_part = tokens.shape
    top_k = expert_ids.shape[1]
    share_rows = hidden_grad.shape[1]
    hidden_units = gate_weight.shape[2]
    capacity = share_rows * n_dp // (n_zh * ZL * CORES)

    n_near = ZL * CORES

    up_rows = lax.all_gather(up_weight, "dp", axis=1, tiled=True)[0]

    def go_out(tokens, expert_ids, gate_weight):
        copies = jnp.broadcast_to(gate_weight, (n_dp, width_part, hidden_units))
        gate_rows = lax.all_to_all(copies, "dp", split_axis=0, concat_axis=0, tiled=True)
        gate_rows = gate_rows.reshape(-1, hidden_units)

        ids_rows = expert_ids.T.astype(jnp.bfloat16)
        sent = jnp.concatenate([tokens, ids_rows], axis=0)
        known = lax.all_gather(sent, "zh", axis=0, tiled=False)
        known_tokens = known[:, :tok_rows]
        known_ids = known[:, tok_rows:].astype(jnp.float32)

        expert_of = lax.axis_index("zh") * n_near + jnp.arange(n_near, dtype=jnp.int32)
        expert_of = expert_of.astype(jnp.float32)[None, :, None]
        hit = jnp.zeros((n_zh, n_near, tok_rows), jnp.bool_)
        for choice_k in range(top_k):
            hit = hit | (known_ids[:, choice_k][:, None] == expert_of)
        earlier = jnp.arange(tok_rows)[:, None] < jnp.arange(tok_rows)[None, :]
        ranks = jnp.dot(
            hit.reshape(-1, tok_rows).astype(jnp.bfloat16),
            earlier.astype(jnp.bfloat16),
            preferred_element_type=jnp.float32,
        ).reshape(hit.shape)
        row_of = jnp.where(hit, ranks.astype(jnp.int32), -1)[:, :, None]
        placer = (
            (row_of == jnp.arange(capacity, dtype=jnp.int32)[:, None])
            .astype(jnp.bfloat16)
            .reshape(n_zh, n_near * capacity, tok_rows)
        )
        outgoing = lax.dot_general(
            placer, known_tokens, (((2,), (1,)), ((0,), (0,))), preferred_element_type=jnp.float32
        ).astype(jnp.bfloat16)
        outgoing = outgoing.reshape(n_zh, n_near, capacity, width_part).transpose(1, 0, 2, 3)
        outgoing, gate_rows = lax.optimization_barrier((outgoing, gate_rows))
        own_width = lax.all_to_all(outgoing, near, split_axis=0, concat_axis=0, tiled=True)
        own_width = own_width.transpose(1, 0, 2, 3)
        by_share = own_width.reshape(n_dp, share_rows, width_part)
        arrived = lax.all_to_all(by_share, "dp", split_axis=0, concat_axis=0, tiled=True)
        return gate_rows, placer, by_share, arrived

    def stay(tokens, expert_ids, gate_weight):
        return (
            jnp.zeros((n_dp * width_part, hidden_units), jnp.bfloat16),
            jnp.zeros((n_zh, n_near * capacity, tok_rows), jnp.bfloat16),
            jnp.zeros((n_dp, share_rows, width_part), jnp.bfloat16),
            jnp.zeros((n_dp, share_rows, width_part), jnp.bfloat16),
        )

    taken = expert_ids[0, 0] >= 0
    gate_rows, placer, by_share, arrived = lax.cond(
        taken, go_out, stay, tokens, expert_ids, gate_weight
    )
    hidden, both_delta, slot_grad = experts(arrived, gate_rows, up_rows, hidden_grad[0])
    all_delta = lax.all_gather(both_delta, "dp", axis=0, tiled=True)
    def go_back(slot_grad, placer):
        back = lax.all_to_all(slot_grad, "dp", split_axis=0, concat_axis=0, tiled=True)
        back = back.reshape(n_zh, n_near, capacity, width_part).transpose(1, 0, 2, 3)
        returned = lax.all_to_all(back, near, split_axis=0, concat_axis=0, tiled=True)
        returned = returned.transpose(1, 0, 2, 3).reshape(n_zh, n_near * capacity, width_part)
        token_sum = lax.dot_general(
            placer, returned, (((1,), (1,)), ((0,), (0,))), preferred_element_type=jnp.float32
        )
        sums = lax.all_to_all(
            token_sum.astype(jnp.bfloat16), "zh", split_axis=0, concat_axis=0, tiled=True
        )
        return jnp.sum(sums.astype(jnp.float32), axis=0).astype(jnp.bfloat16)

    token_grad = lax.cond(
        taken, go_back, lambda *_: jnp.zeros_like(tokens), slot_grad, placer
    )

    gate_grad, up_grad = weight_grads(by_share, all_delta)
    return hidden[None], gate_grad[None], up_grad[None], token_grad


def solution(mesh):
    n_expert, n_dp = mesh.devices.shape
    split = Mesh(mesh.devices.reshape(n_expert // (ZL * CORES), ZL, CORES, n_dp), ("zh", "zl", "c", "dp"))
    expert = ("zh", "zl", "c")
    placed = (
        P(expert, "dp"),
        P(expert, None),
        P(expert, "dp", None),
        P(expert, "dp", None),
        P(expert, "dp", None),
    )
    return jax.shard_map(
        on_device,
        mesh=split,
        in_specs=placed,
        out_specs=(
            P(expert, "dp", None),
            P(expert, "dp", None),
            P(expert, "dp", None),
            P(expert, "dp"),
        ),
        check_vma=False,
    )
```

```python
import jax
import jax.numpy as jnp
from jax import lax
from jax.experimental import pallas as pl
from jax.experimental.pallas import tpu as pltpu
from jax.sharding import Mesh, PartitionSpec as P

CORES = 2
ZL = 4
DP_X = 4


def expert_kernel(rows_ref, weights_ref, grad_ref, hidden_ref, delta_ref, slot_grad_ref):
    n_dp, _, width_part = rows_ref.shape
    hidden_units = grad_ref.shape[1]
    rows = jnp.concatenate([rows_ref[part] for part in range(n_dp)], axis=1)
    both = jnp.dot(rows, weights_ref[...], preferred_element_type=jnp.float32)
    gate, up = both[:, :hidden_units], both[:, hidden_units:]
    sigmoid_gate = jax.nn.sigmoid(gate)
    silu_gate = gate * sigmoid_gate
    hidden_ref[...] = (silu_gate * up).astype(jnp.bfloat16)
    grad = grad_ref[...].astype(jnp.float32)
    delta_ref[:, :hidden_units] = (
        grad * up * sigmoid_gate * (1.0 + gate * (1.0 - sigmoid_gate))
    ).astype(jnp.bfloat16)
    delta_ref[:, hidden_units:] = (grad * silu_gate).astype(jnp.bfloat16)
    delta = delta_ref[...]
    for part in range(n_dp):
        slot_grad_ref[part] = lax.dot_general(
            delta,
            weights_ref[part * width_part : (part + 1) * width_part],
            (((1,), (1,)), ((), ())),
            preferred_element_type=jnp.float32,
        ).astype(jnp.bfloat16)


def experts(rows, weights, grad):
    n_dp, share_rows, width_part = rows.shape
    both_units = weights.shape[1]
    flops = 4 * share_rows * n_dp * width_part * both_units
    return pl.pallas_call(
        expert_kernel,
        out_shape=(
            jax.ShapeDtypeStruct((share_rows, both_units // 2), jnp.bfloat16),
            jax.ShapeDtypeStruct((share_rows, both_units), jnp.bfloat16),
            jax.ShapeDtypeStruct(rows.shape, jnp.bfloat16),
        ),
        compiler_params=pltpu.CompilerParams(vmem_limit_bytes=32 * 1024 * 1024),
        cost_estimate=pl.CostEstimate(
            flops=flops, bytes_accessed=2 * weights.size, transcendentals=grad.size
        ),
    )(rows, weights, grad)


def copies_kernel(gate_ref, up_ref, out_ref, rows, sems):
    hidden_units = gate_ref.shape[2]
    rows[:, :hidden_units] = gate_ref[0]
    rows[:, hidden_units:] = up_ref[0]
    copies = [
        pltpu.make_async_copy(rows, out_ref.at[part], sems.at[part])
        for part in range(out_ref.shape[0])
    ]
    for copy in copies:
        copy.start()
    for copy in copies:
        copy.wait()


def weight_copies(gate_w, up_w, n_dp):
    _, rows, hidden_units = gate_w.shape
    return pl.pallas_call(
        copies_kernel,
        out_shape=jax.ShapeDtypeStruct((n_dp, rows, 2 * hidden_units), gate_w.dtype),
        out_specs=pl.BlockSpec(memory_space=pl.ANY),
        scratch_shapes=[
            pltpu.VMEM((rows, 2 * hidden_units), gate_w.dtype),
            pltpu.SemaphoreType.DMA((n_dp,)),
        ],
    )(gate_w, up_w)


def weight_grad_kernel(order_ref, rows_ref, *refs):
    delta_refs, (gate_grad_ref, up_grad_ref) = refs[:-2], refs[-2:]
    share_rows = rows_ref.shape[1]
    hidden_units = gate_grad_ref.shape[1]
    n_x = rows_ref.shape[0] // len(delta_refs)
    total = jnp.zeros((rows_ref.shape[2], 2 * hidden_units), jnp.float32)
    for block, delta_ref in enumerate(delta_refs):
        rows = jnp.concatenate(
            [rows_ref[order_ref[block * n_x + part]] for part in range(n_x)], axis=0
        )
        total = total + lax.dot_general(
            rows, delta_ref[...], (((0,), (0,)), ((), ())), preferred_element_type=jnp.float32
        )
    gate_grad_ref[...] = total[:, :hidden_units]
    up_grad_ref[...] = total[:, hidden_units:]


def weight_grads(order, rows, deltas):
    both_units = deltas[0].shape[1]
    out = jax.ShapeDtypeStruct((rows.shape[2], both_units // 2), jnp.float32)
    in_vmem = pl.BlockSpec(memory_space=pltpu.VMEM)
    return pl.pallas_call(
        weight_grad_kernel,
        in_specs=[pl.BlockSpec(memory_space=pltpu.SMEM)] + [in_vmem] * (1 + len(deltas)),
        out_shape=(out, out),
        compiler_params=pltpu.CompilerParams(vmem_limit_bytes=32 * 1024 * 1024),
        cost_estimate=pl.CostEstimate(
            flops=2 * rows.size * both_units, bytes_accessed=2 * rows.size, transcendentals=0
        ),
    )(order, rows, *deltas)


def blocks_along(block, axis):
    n = lax.axis_size(axis)
    steps = [[(i, (i - k) % n) for i in range(n)] for k in range(1, n)]
    return [block] + [lax.ppermute(block, axis, step) for step in steps]


def on_device(tokens, expert_ids, gate_weight, up_weight, hidden_grad):
    n_zh = lax.axis_size("zh")
    dp = ("x", "y")
    n_x, n_y = lax.axis_size("x"), lax.axis_size("y")
    n_dp = n_x * n_y
    near = ("zl", "c")
    tok_rows, width_part = tokens.shape
    top_k = expert_ids.shape[1]
    share_rows = hidden_grad.shape[1]
    hidden_units = gate_weight.shape[2]
    capacity = share_rows * n_dp // (n_zh * ZL * CORES)

    weights = weight_copies(gate_weight, up_weight, n_dp)
    weights = lax.all_to_all(weights, dp, split_axis=0, concat_axis=0, tiled=True)
    weights = weights.reshape(-1, 2 * hidden_units)

    ids_rows = expert_ids.T.astype(jnp.bfloat16)
    sent = jnp.concatenate([tokens, ids_rows], axis=0)
    known = lax.all_gather(sent, "zh", axis=0, tiled=False)
    known_tokens = known[:, :tok_rows]
    known_ids = known[:, tok_rows:].astype(jnp.float32)

    n_near = ZL * CORES
    expert_of = lax.axis_index("zh") * n_near + jnp.arange(n_near, dtype=jnp.int32)
    expert_of = expert_of.astype(jnp.float32)[None, :, None]
    hit = jnp.zeros((n_zh, n_near, tok_rows), jnp.bool_)
    for choice_k in range(top_k):
        hit = hit | (known_ids[:, choice_k][:, None] == expert_of)
    earlier = jnp.arange(tok_rows)[:, None] < jnp.arange(tok_rows)[None, :]
    ranks = jnp.dot(
        hit.reshape(-1, tok_rows).astype(jnp.bfloat16),
        earlier.astype(jnp.bfloat16),
        preferred_element_type=jnp.float32,
    ).reshape(hit.shape)
    row_of = jnp.where(hit, ranks.astype(jnp.int32), -1)[:, :, None]
    placer = (
        (row_of == jnp.arange(capacity, dtype=jnp.int32)[:, None])
        .astype(jnp.bfloat16)
        .reshape(n_zh, n_near * capacity, tok_rows)
    )
    outgoing = lax.dot_general(
        placer, known_tokens, (((2,), (1,)), ((0,), (0,))), preferred_element_type=jnp.float32
    ).astype(jnp.bfloat16)
    outgoing = outgoing.reshape(n_zh, n_near, capacity, width_part).transpose(1, 0, 2, 3)
    outgoing, weights = lax.optimization_barrier((outgoing, weights))
    own_width = lax.all_to_all(outgoing, near, split_axis=0, concat_axis=0, tiled=True)
    own_width = own_width.transpose(1, 0, 2, 3)
    by_share = own_width.reshape(n_dp, share_rows, width_part)
    arrived = lax.all_to_all(by_share, dp, split_axis=0, concat_axis=0, tiled=True)
    hidden, both_delta, slot_grad = experts(arrived, weights, hidden_grad[0])

    def swap_shares(slot_grad):
        return lax.all_to_all(slot_grad, dp, split_axis=0, concat_axis=0, tiled=True)

    def go_back(back, placer):
        back = back.reshape(n_zh, n_near, capacity, width_part).transpose(1, 0, 2, 3)
        returned = lax.all_to_all(back, near, split_axis=0, concat_axis=0, tiled=True)
        returned = returned.transpose(1, 0, 2, 3).reshape(n_zh, n_near * capacity, width_part)
        token_sum = lax.dot_general(
            placer, returned, (((1,), (1,)), ((0,), (0,))), preferred_element_type=jnp.float32
        )
        sums = lax.all_to_all(
            token_sum.astype(jnp.bfloat16), "zh", split_axis=0, concat_axis=0, tiled=True
        )
        return jnp.sum(sums.astype(jnp.float32), axis=0).astype(jnp.bfloat16)

    taken = expert_ids[0, 0] >= 0
    along_x = jnp.concatenate(blocks_along(both_delta, "x"), axis=0)
    back = lax.cond(taken, swap_shares, jnp.zeros_like, slot_grad)
    along_x, back = lax.optimization_barrier((along_x, back))
    deltas = blocks_along(along_x, "y")
    token_grad = lax.cond(taken, go_back, lambda *_: jnp.zeros_like(tokens), back, placer)

    place_x = (lax.axis_index("x") + jnp.arange(n_x, dtype=jnp.int32)) % n_x
    place_y = (lax.axis_index("y") + jnp.arange(n_y, dtype=jnp.int32)) % n_y
    order = (place_x[None, :] * n_y + place_y[:, None]).reshape(n_dp)
    gate_grad, up_grad = weight_grads(order, by_share, deltas)
    return hidden[None], gate_grad[None], up_grad[None], token_grad


def solution(mesh):
    n_expert, n_dp = mesh.devices.shape
    split = Mesh(
        mesh.devices.reshape(n_expert // (ZL * CORES), ZL, CORES, DP_X, n_dp // DP_X),
        ("zh", "zl", "c", "x", "y"),
    )
    expert, dp = ("zh", "zl", "c"), ("x", "y")
    placed = (
        P(expert, dp),
        P(expert, None),
        P(expert, dp, None),
        P(expert, dp, None),
        P(expert, dp, None),
    )
    return jax.shard_map(
        on_device,
        mesh=split,
        in_specs=placed,
        out_specs=(
            P(expert, dp, None),
            P(expert, dp, None),
            P(expert, dp, None),
            P(expert, dp),
        ),
        check_vma=False,
    )
```

```python
import jax
import jax.numpy as jnp
from jax import lax
from jax.experimental import pallas as pl
from jax.experimental.pallas import tpu as pltpu
from jax.sharding import Mesh, PartitionSpec as P

CORES = 2
ZL = 4
DP_X = 4


def expert_kernel(rows_ref, weights_ref, grad_ref, hidden_ref, delta_ref, slot_grad_ref):
    n_dp, _, width_part = rows_ref.shape
    hidden_units = grad_ref.shape[1]
    rows = jnp.concatenate([rows_ref[part] for part in range(n_dp)], axis=1)
    both = jnp.dot(rows, weights_ref[...], preferred_element_type=jnp.float32)
    gate, up = both[:, :hidden_units], both[:, hidden_units:]
    sigmoid_gate = jax.nn.sigmoid(gate)
    silu_gate = gate * sigmoid_gate
    hidden_ref[...] = (silu_gate * up).astype(jnp.bfloat16)
    grad = grad_ref[...].astype(jnp.float32)
    delta_ref[:, :hidden_units] = (
        grad * up * sigmoid_gate * (1.0 + gate * (1.0 - sigmoid_gate))
    ).astype(jnp.bfloat16)
    delta_ref[:, hidden_units:] = (grad * silu_gate).astype(jnp.bfloat16)
    delta = delta_ref[...]
    for part in range(n_dp):
        slot_grad_ref[part] = lax.dot_general(
            delta,
            weights_ref[part * width_part : (part + 1) * width_part],
            (((1,), (1,)), ((), ())),
            preferred_element_type=jnp.float32,
        ).astype(jnp.bfloat16)


def experts(rows, weights, grad):
    n_dp, share_rows, width_part = rows.shape
    both_units = weights.shape[1]
    flops = 4 * share_rows * n_dp * width_part * both_units
    return pl.pallas_call(
        expert_kernel,
        out_shape=(
            jax.ShapeDtypeStruct((share_rows, both_units // 2), jnp.bfloat16),
            jax.ShapeDtypeStruct((share_rows, both_units), jnp.bfloat16),
            jax.ShapeDtypeStruct(rows.shape, jnp.bfloat16),
        ),
        compiler_params=pltpu.CompilerParams(vmem_limit_bytes=32 * 1024 * 1024),
        cost_estimate=pl.CostEstimate(
            flops=flops, bytes_accessed=2 * weights.size, transcendentals=grad.size
        ),
    )(rows, weights, grad)


def copies_kernel(gate_ref, up_ref, out_ref, rows, sems):
    hidden_units = gate_ref.shape[2]
    rows[:, :hidden_units] = gate_ref[0]
    rows[:, hidden_units:] = up_ref[0]
    copies = [
        pltpu.make_async_copy(rows, out_ref.at[part], sems.at[part])
        for part in range(out_ref.shape[0])
    ]
    for copy in copies:
        copy.start()
    for copy in copies:
        copy.wait()


def weight_copies(gate_w, up_w, n_dp):
    _, rows, hidden_units = gate_w.shape
    return pl.pallas_call(
        copies_kernel,
        out_shape=jax.ShapeDtypeStruct((n_dp, rows, 2 * hidden_units), gate_w.dtype),
        out_specs=pl.BlockSpec(memory_space=pl.ANY),
        scratch_shapes=[
            pltpu.VMEM((rows, 2 * hidden_units), gate_w.dtype),
            pltpu.SemaphoreType.DMA((n_dp,)),
        ],
    )(gate_w, up_w)


def weight_grad_kernel(order_ref, rows_ref, *refs):
    delta_refs, (gate_grad_ref, up_grad_ref) = refs[:-2], refs[-2:]
    share_rows = rows_ref.shape[1]
    hidden_units = gate_grad_ref.shape[1]
    n_x = rows_ref.shape[0] // len(delta_refs)
    total = jnp.zeros((rows_ref.shape[2], 2 * hidden_units), jnp.float32)
    for block, delta_ref in enumerate(delta_refs):
        rows = jnp.concatenate(
            [rows_ref[order_ref[block * n_x + part]] for part in range(n_x)], axis=0
        )
        total = total + lax.dot_general(
            rows, delta_ref[...], (((0,), (0,)), ((), ())), preferred_element_type=jnp.float32
        )
    gate_grad_ref[...] = total[:, :hidden_units]
    up_grad_ref[...] = total[:, hidden_units:]


def weight_grads(order, rows, deltas):
    both_units = deltas[0].shape[1]
    out = jax.ShapeDtypeStruct((rows.shape[2], both_units // 2), jnp.float32)
    in_vmem = pl.BlockSpec(memory_space=pltpu.VMEM)
    return pl.pallas_call(
        weight_grad_kernel,
        in_specs=[pl.BlockSpec(memory_space=pltpu.SMEM)] + [in_vmem] * (1 + len(deltas)),
        out_shape=(out, out),
        compiler_params=pltpu.CompilerParams(vmem_limit_bytes=32 * 1024 * 1024),
        cost_estimate=pl.CostEstimate(
            flops=2 * rows.size * both_units, bytes_accessed=2 * rows.size, transcendentals=0
        ),
    )(order, rows, *deltas)


def blocks_along(block, axis):
    n = lax.axis_size(axis)
    steps = [[(i, (i - k) % n) for i in range(n)] for k in range(1, n)]
    return [block] + [lax.ppermute(block, axis, step) for step in steps]


def on_device(tokens, expert_ids, gate_weight, up_weight, hidden_grad):
    n_zh = lax.axis_size("zh")
    dp = ("x", "y")
    n_x, n_y = lax.axis_size("x"), lax.axis_size("y")
    n_dp = n_x * n_y
    near = ("zl", "c")
    tok_rows, width_part = tokens.shape
    top_k = expert_ids.shape[1]
    share_rows = hidden_grad.shape[1]
    hidden_units = gate_weight.shape[2]
    capacity = share_rows * n_dp // (n_zh * ZL * CORES)

    weights = weight_copies(gate_weight, up_weight, n_dp)
    weights = lax.all_to_all(weights, dp, split_axis=0, concat_axis=0, tiled=True)
    weights = weights.reshape(-1, 2 * hidden_units)

    ids_rows = expert_ids.T.astype(jnp.bfloat16)
    sent = jnp.concatenate([tokens, ids_rows], axis=0)
    known = lax.all_gather(sent, "zh", axis=0, tiled=False)
    known_tokens = known[:, :tok_rows]
    known_ids = known[:, tok_rows:].astype(jnp.float32)

    n_near = ZL * CORES
    expert_of = lax.axis_index("zh") * n_near + jnp.arange(n_near, dtype=jnp.int32)
    expert_of = expert_of.astype(jnp.float32)[None, :, None]
    hit = jnp.zeros((n_zh, n_near, tok_rows), jnp.bool_)
    for choice_k in range(top_k):
        hit = hit | (known_ids[:, choice_k][:, None] == expert_of)
    earlier = jnp.arange(tok_rows)[:, None] < jnp.arange(tok_rows)[None, :]
    ranks = jnp.dot(
        hit.reshape(-1, tok_rows).astype(jnp.bfloat16),
        earlier.astype(jnp.bfloat16),
        preferred_element_type=jnp.float32,
    ).reshape(hit.shape)
    row_of = jnp.where(hit, ranks.astype(jnp.int32), -1)[:, :, None]
    placer = (
        (row_of == jnp.arange(capacity, dtype=jnp.int32)[:, None])
        .astype(jnp.bfloat16)
        .reshape(n_zh, n_near * capacity, tok_rows)
    )
    outgoing = lax.dot_general(
        placer, known_tokens, (((2,), (1,)), ((0,), (0,))), preferred_element_type=jnp.float32
    ).astype(jnp.bfloat16)
    outgoing = outgoing.reshape(n_zh, n_near, capacity, width_part).transpose(1, 0, 2, 3)
    outgoing, weights = lax.optimization_barrier((outgoing, weights))
    own_width = lax.all_to_all(outgoing, near, split_axis=0, concat_axis=0, tiled=True)
    own_width = own_width.transpose(1, 0, 2, 3)
    by_share = own_width.reshape(n_dp, share_rows, width_part)
    arrived = lax.all_to_all(by_share, dp, split_axis=0, concat_axis=0, tiled=True)
    hidden, both_delta, slot_grad = experts(arrived, weights, hidden_grad[0])

    def swap_shares(slot_grad):
        return lax.all_to_all(slot_grad, dp, split_axis=0, concat_axis=0, tiled=True)

    def go_near(back):
        back = back.reshape(n_zh, n_near, capacity, width_part).transpose(1, 0, 2, 3)
        returned = lax.all_to_all(back, near, split_axis=0, concat_axis=0, tiled=True)
        return returned.reshape(slot_grad.shape)

    def go_home(returned, placer):
        returned = returned.reshape(n_near, n_zh, capacity, width_part).transpose(1, 0, 2, 3)
        token_sum = lax.dot_general(
            placer,
            returned.reshape(n_zh, n_near * capacity, width_part),
            (((1,), (1,)), ((0,), (0,))),
            preferred_element_type=jnp.float32,
        )
        sums = lax.all_to_all(
            token_sum.astype(jnp.bfloat16), "zh", split_axis=0, concat_axis=0, tiled=True
        )
        return jnp.sum(sums.astype(jnp.float32), axis=0).astype(jnp.bfloat16)

    taken = expert_ids[0, 0] >= 0
    along_x = both_delta
    step = 1
    for window in (swap_shares, go_near):
        if step < n_x:
            pair = [(i, i ^ step) for i in range(n_x)]
            along_x = jnp.concatenate([along_x, lax.ppermute(along_x, "x", pair)], axis=0)
            step *= 2
        slot_grad = lax.cond(taken, window, jnp.zeros_like, slot_grad)
        along_x, slot_grad = lax.optimization_barrier((along_x, slot_grad))
    deltas = blocks_along(along_x, "y")
    token_grad = lax.cond(taken, go_home, lambda *_: jnp.zeros_like(tokens), slot_grad, placer)

    place_x = lax.axis_index("x") ^ jnp.arange(n_x, dtype=jnp.int32)
    place_y = (lax.axis_index("y") + jnp.arange(n_y, dtype=jnp.int32)) % n_y
    order = (place_x[None, :] * n_y + place_y[:, None]).reshape(n_dp)
    gate_grad, up_grad = weight_grads(order, by_share, deltas)
    return hidden[None], gate_grad[None], up_grad[None], token_grad


def solution(mesh):
    n_expert, n_dp = mesh.devices.shape
    split = Mesh(
        mesh.devices.reshape(n_expert // (ZL * CORES), ZL, CORES, DP_X, n_dp // DP_X),
        ("zh", "zl", "c", "x", "y"),
    )
    expert, dp = ("zh", "zl", "c"), ("x", "y")
    placed = (
        P(expert, dp),
        P(expert, None),
        P(expert, dp, None),
        P(expert, dp, None),
        P(expert, dp, None),
    )
    return jax.shard_map(
        on_device,
        mesh=split,
        in_specs=placed,
        out_specs=(
            P(expert, dp, None),
            P(expert, dp, None),
            P(expert, dp, None),
            P(expert, dp),
        ),
        check_vma=False,
    )
```

```python
import jax
import jax.numpy as jnp
from jax import lax
from jax.experimental import pallas as pl
from jax.experimental.pallas import tpu as pltpu
from jax.sharding import Mesh, PartitionSpec as P

CORES = 2
ZL = 4
X_HIGH, X_LOW = 2, 2


def expert_kernel(rows_ref, weights_ref, grad_ref, hidden_ref, delta_ref, slot_grad_ref):
    n_dp, _, width_part = rows_ref.shape
    hidden_units = grad_ref.shape[1]
    rows = jnp.concatenate([rows_ref[part] for part in range(n_dp)], axis=1)
    both = jnp.dot(rows, weights_ref[...], preferred_element_type=jnp.float32)
    gate, up = both[:, :hidden_units], both[:, hidden_units:]
    sigmoid_gate = jax.nn.sigmoid(gate)
    silu_gate = gate * sigmoid_gate
    hidden_ref[...] = (silu_gate * up).astype(jnp.bfloat16)
    grad = grad_ref[...].astype(jnp.float32)
    delta_ref[:, :hidden_units] = (
        grad * up * sigmoid_gate * (1.0 + gate * (1.0 - sigmoid_gate))
    ).astype(jnp.bfloat16)
    delta_ref[:, hidden_units:] = (grad * silu_gate).astype(jnp.bfloat16)
    delta = delta_ref[...]
    for part in range(n_dp):
        slot_grad_ref[part] = lax.dot_general(
            delta,
            weights_ref[part * width_part : (part + 1) * width_part],
            (((1,), (1,)), ((), ())),
            preferred_element_type=jnp.float32,
        ).astype(jnp.bfloat16)


def experts(rows, weights, grad):
    n_dp, share_rows, width_part = rows.shape
    both_units = weights.shape[1]
    flops = 4 * share_rows * n_dp * width_part * both_units
    return pl.pallas_call(
        expert_kernel,
        out_shape=(
            jax.ShapeDtypeStruct((share_rows, both_units // 2), jnp.bfloat16),
            jax.ShapeDtypeStruct((share_rows, both_units), jnp.bfloat16),
            jax.ShapeDtypeStruct(rows.shape, jnp.bfloat16),
        ),
        compiler_params=pltpu.CompilerParams(vmem_limit_bytes=32 * 1024 * 1024),
        cost_estimate=pl.CostEstimate(
            flops=flops, bytes_accessed=2 * weights.size, transcendentals=grad.size
        ),
    )(rows, weights, grad)


def copies_kernel(gate_ref, up_ref, out_ref, rows, sems):
    hidden_units = gate_ref.shape[2]
    rows[:, :hidden_units] = gate_ref[0]
    rows[:, hidden_units:] = up_ref[0]
    copies = [
        pltpu.make_async_copy(rows, out_ref.at[part], sems.at[part])
        for part in range(out_ref.shape[0])
    ]
    for copy in copies:
        copy.start()
    for copy in copies:
        copy.wait()


def weight_copies(gate_w, up_w, n_dp):
    _, rows, hidden_units = gate_w.shape
    return pl.pallas_call(
        copies_kernel,
        out_shape=jax.ShapeDtypeStruct((n_dp, rows, 2 * hidden_units), gate_w.dtype),
        out_specs=pl.BlockSpec(memory_space=pl.ANY),
        scratch_shapes=[
            pltpu.VMEM((rows, 2 * hidden_units), gate_w.dtype),
            pltpu.SemaphoreType.DMA((n_dp,)),
        ],
    )(gate_w, up_w)


def on_device(tokens, expert_ids, gate_weight, up_weight, hidden_grad):
    n_zh = lax.axis_size("zh")
    dp = ("xh", "xl", "y")
    n_dp = lax.axis_size(dp)
    near = ("zl", "c")
    tok_rows, width_part = tokens.shape
    top_k = expert_ids.shape[1]
    share_rows = hidden_grad.shape[1]
    hidden_units = gate_weight.shape[2]
    capacity = share_rows * n_dp // (n_zh * ZL * CORES)

    weights = weight_copies(gate_weight, up_weight, n_dp)
    weights = lax.all_to_all(weights, dp, split_axis=0, concat_axis=0, tiled=True)
    weights = weights.reshape(-1, 2 * hidden_units)

    ids_rows = expert_ids.T.astype(jnp.bfloat16)
    sent = jnp.concatenate([tokens, ids_rows], axis=0)
    known = lax.all_gather(sent, "zh", axis=0, tiled=False)
    known_tokens = known[:, :tok_rows]
    known_ids = known[:, tok_rows:].astype(jnp.float32)

    n_near = ZL * CORES
    expert_of = lax.axis_index("zh") * n_near + jnp.arange(n_near, dtype=jnp.int32)
    expert_of = expert_of.astype(jnp.float32)[None, :, None]
    hit = jnp.zeros((n_zh, n_near, tok_rows), jnp.bool_)
    for choice_k in range(top_k):
        hit = hit | (known_ids[:, choice_k][:, None] == expert_of)
    earlier = jnp.arange(tok_rows)[:, None] < jnp.arange(tok_rows)[None, :]
    ranks = jnp.dot(
        hit.reshape(-1, tok_rows).astype(jnp.bfloat16),
        earlier.astype(jnp.bfloat16),
        preferred_element_type=jnp.float32,
    ).reshape(hit.shape)
    row_of = jnp.where(hit, ranks.astype(jnp.int32), -1)[:, :, None]
    placer = (
        (row_of == jnp.arange(capacity, dtype=jnp.int32)[:, None])
        .astype(jnp.bfloat16)
        .reshape(n_zh, n_near * capacity, tok_rows)
    )
    outgoing = lax.dot_general(
        placer, known_tokens, (((2,), (1,)), ((0,), (0,))), preferred_element_type=jnp.float32
    ).astype(jnp.bfloat16)
    outgoing = outgoing.reshape(n_zh, n_near, capacity, width_part).transpose(1, 0, 2, 3)
    outgoing, weights = lax.optimization_barrier((outgoing, weights))
    own_width = lax.all_to_all(outgoing, near, split_axis=0, concat_axis=0, tiled=True)
    own_width = own_width.transpose(1, 0, 2, 3)
    by_share = own_width.reshape(n_dp, share_rows, width_part)
    arrived = lax.all_to_all(by_share, dp, split_axis=0, concat_axis=0, tiled=True)
    hidden, both_delta, slot_grad = experts(arrived, weights, hidden_grad[0])

    def swap_shares(slot_grad):
        return lax.all_to_all(slot_grad, dp, split_axis=0, concat_axis=0, tiled=True)

    def go_back(back, placer):
        back = back.reshape(n_zh, n_near, capacity, width_part).transpose(1, 0, 2, 3)
        returned = lax.all_to_all(back, near, split_axis=0, concat_axis=0, tiled=True)
        returned = returned.transpose(1, 0, 2, 3).reshape(n_zh, n_near * capacity, width_part)
        token_sum = lax.dot_general(
            placer, returned, (((1,), (1,)), ((0,), (0,))), preferred_element_type=jnp.float32
        )
        sums = lax.all_to_all(
            token_sum.astype(jnp.bfloat16), "zh", split_axis=0, concat_axis=0, tiled=True
        )
        return jnp.sum(sums.astype(jnp.float32), axis=0).astype(jnp.bfloat16)

    taken = expert_ids[0, 0] >= 0
    other_delta = lax.ppermute(both_delta, "xl", [(0, 1), (1, 0)])
    back = lax.cond(taken, swap_shares, jnp.zeros_like, slot_grad)
    other_delta, back = lax.optimization_barrier((other_delta, back))
    low = lax.axis_index("xl") == 0
    pair_delta = jnp.concatenate(
        [jnp.where(low, both_delta, other_delta), jnp.where(low, other_delta, both_delta)], axis=0
    )
    pair_delta, back = lax.optimization_barrier((pair_delta, back))
    all_delta = lax.all_gather(pair_delta, ("xh", "y"), axis=0, tiled=True)
    token_grad = lax.cond(taken, go_back, lambda *_: jnp.zeros_like(tokens), back, placer)

    ordered = by_share.reshape(
        lax.axis_size("xh"), X_LOW, lax.axis_size("y"), share_rows, width_part
    ).transpose(0, 2, 1, 3, 4)
    both_grad = lax.dot_general(
        ordered.reshape(n_dp * share_rows, width_part),
        all_delta,
        (((0,), (0,)), ((), ())),
        preferred_element_type=jnp.float32,
    )
    return (
        hidden[None],
        both_grad[None, :, :hidden_units],
        both_grad[None, :, hidden_units:],
        token_grad,
    )


def solution(mesh):
    n_expert, n_dp = mesh.devices.shape
    split = Mesh(
        mesh.devices.reshape(
            n_expert // (ZL * CORES), ZL, CORES, X_HIGH, X_LOW, n_dp // (X_HIGH * X_LOW)
        ),
        ("zh", "zl", "c", "xh", "xl", "y"),
    )
    expert, dp = ("zh", "zl", "c"), ("xh", "xl", "y")
    placed = (
        P(expert, dp),
        P(expert, None),
        P(expert, dp, None),
        P(expert, dp, None),
        P(expert, dp, None),
    )
    return jax.shard_map(
        on_device,
        mesh=split,
        in_specs=placed,
        out_specs=(
            P(expert, dp, None),
            P(expert, dp, None),
            P(expert, dp, None),
            P(expert, dp),
        ),
        check_vma=False,
    )
```

```python
import jax
import jax.numpy as jnp
from jax import lax
from jax.experimental import pallas as pl
from jax.experimental.pallas import tpu as pltpu
from jax.sharding import Mesh, PartitionSpec as P

CORES = 2
ZL = 4


def expert_kernel(rows_ref, weights_ref, grad_ref, hidden_ref, delta_ref):
    n_dp = rows_ref.shape[0]
    hidden_units = grad_ref.shape[1]
    rows = jnp.concatenate([rows_ref[part] for part in range(n_dp)], axis=1)
    both = jnp.dot(rows, weights_ref[...], preferred_element_type=jnp.float32)
    gate, up = both[:, :hidden_units], both[:, hidden_units:]
    sigmoid_gate = jax.nn.sigmoid(gate)
    silu_gate = gate * sigmoid_gate
    hidden_ref[...] = (silu_gate * up).astype(jnp.bfloat16)
    grad = grad_ref[...].astype(jnp.float32)
    delta_ref[:, :hidden_units] = (
        grad * up * sigmoid_gate * (1.0 + gate * (1.0 - sigmoid_gate))
    ).astype(jnp.bfloat16)
    delta_ref[:, hidden_units:] = (grad * silu_gate).astype(jnp.bfloat16)


def experts(rows, weights, grad):
    share_rows, hidden_units = grad.shape
    return pl.pallas_call(
        expert_kernel,
        out_shape=(
            jax.ShapeDtypeStruct((share_rows, hidden_units), jnp.bfloat16),
            jax.ShapeDtypeStruct((share_rows, 2 * hidden_units), jnp.bfloat16),
        ),
        compiler_params=pltpu.CompilerParams(vmem_limit_bytes=32 * 1024 * 1024),
        cost_estimate=pl.CostEstimate(
            flops=2 * share_rows * weights.size,
            bytes_accessed=2 * weights.size,
            transcendentals=grad.size,
        ),
    )(rows, weights, grad)


def slot_grad_kernel(delta_ref, weights_ref, slot_grad_ref):
    n_dp, _, width_part = slot_grad_ref.shape
    delta = delta_ref[...]
    for part in range(n_dp):
        slot_grad_ref[part] = lax.dot_general(
            delta,
            weights_ref[part * width_part : (part + 1) * width_part],
            (((1,), (1,)), ((), ())),
            preferred_element_type=jnp.float32,
        ).astype(jnp.bfloat16)


def slot_grads(delta, weights, n_dp):
    share_rows = delta.shape[0]
    return pl.pallas_call(
        slot_grad_kernel,
        out_shape=jax.ShapeDtypeStruct(
            (n_dp, share_rows, weights.shape[0] // n_dp), jnp.bfloat16
        ),
        compiler_params=pltpu.CompilerParams(vmem_limit_bytes=32 * 1024 * 1024),
        cost_estimate=pl.CostEstimate(
            flops=2 * share_rows * weights.size,
            bytes_accessed=2 * weights.size,
            transcendentals=0,
        ),
    )(delta, weights)


def copies_kernel(gate_ref, up_ref, out_ref, rows, sems):
    hidden_units = gate_ref.shape[2]
    rows[:, :hidden_units] = gate_ref[0]
    rows[:, hidden_units:] = up_ref[0]
    copies = [
        pltpu.make_async_copy(rows, out_ref.at[part], sems.at[part])
        for part in range(out_ref.shape[0])
    ]
    for copy in copies:
        copy.start()
    for copy in copies:
        copy.wait()


def weight_copies(gate_w, up_w, n_dp):
    _, rows, hidden_units = gate_w.shape
    return pl.pallas_call(
        copies_kernel,
        out_shape=jax.ShapeDtypeStruct((n_dp, rows, 2 * hidden_units), gate_w.dtype),
        out_specs=pl.BlockSpec(memory_space=pl.ANY),
        scratch_shapes=[
            pltpu.VMEM((rows, 2 * hidden_units), gate_w.dtype),
            pltpu.SemaphoreType.DMA((n_dp,)),
        ],
    )(gate_w, up_w)


def weight_grad_kernel(rows_ref, delta_ref, gate_grad_ref, up_grad_ref):
    hidden_units = gate_grad_ref.shape[1]

    @pl.when(pl.program_id(0) == 0)
    def _():
        gate_grad_ref[...] = jnp.zeros_like(gate_grad_ref)
        up_grad_ref[...] = jnp.zeros_like(up_grad_ref)

    both = jnp.dot(rows_ref[...], delta_ref[...], preferred_element_type=jnp.float32)
    gate_grad_ref[...] += both[:, :hidden_units]
    up_grad_ref[...] += both[:, hidden_units:]


def weight_grads(rows, delta):
    width_part, slots = rows.shape
    both_units = delta.shape[1]
    step = slots // 4
    out = jax.ShapeDtypeStruct((width_part, both_units // 2), jnp.float32)
    out_spec = pl.BlockSpec((width_part, both_units // 2), lambda i: (0, 0))
    return pl.pallas_call(
        weight_grad_kernel,
        grid=(slots // step,),
        in_specs=[
            pl.BlockSpec((width_part, step), lambda i: (0, i)),
            pl.BlockSpec((step, both_units), lambda i: (i, 0)),
        ],
        out_specs=(out_spec, out_spec),
        out_shape=(out, out),
        cost_estimate=pl.CostEstimate(
            flops=2 * rows.size * both_units, bytes_accessed=2 * delta.size, transcendentals=0
        ),
    )(rows, delta)


def on_device(tokens, expert_ids, gate_weight, up_weight, hidden_grad):
    n_zh = lax.axis_size("zh")
    n_dp = lax.axis_size("dp")
    near = ("zl", "c")
    tok_rows, width_part = tokens.shape
    top_k = expert_ids.shape[1]
    share_rows = hidden_grad.shape[1]
    hidden_units = gate_weight.shape[2]
    capacity = share_rows * n_dp // (n_zh * ZL * CORES)

    weights = weight_copies(gate_weight, up_weight, n_dp)
    weights = lax.all_to_all(weights, "dp", split_axis=0, concat_axis=0, tiled=True)
    weights = weights.reshape(-1, 2 * hidden_units)

    ids_rows = expert_ids.T.astype(jnp.bfloat16)
    sent = jnp.concatenate([tokens, ids_rows], axis=0)
    known = lax.all_gather(sent, "zh", axis=0, tiled=False)
    known_tokens = known[:, :tok_rows]
    known_ids = known[:, tok_rows:].astype(jnp.float32)

    n_near = ZL * CORES
    expert_of = lax.axis_index("zh") * n_near + jnp.arange(n_near, dtype=jnp.int32)
    expert_of = expert_of.astype(jnp.float32)[None, :, None]
    hit = jnp.zeros((n_zh, n_near, tok_rows), jnp.bool_)
    for choice_k in range(top_k):
        hit = hit | (known_ids[:, choice_k][:, None] == expert_of)
    earlier = jnp.arange(tok_rows)[:, None] < jnp.arange(tok_rows)[None, :]
    ranks = jnp.dot(
        hit.reshape(-1, tok_rows).astype(jnp.bfloat16),
        earlier.astype(jnp.bfloat16),
        preferred_element_type=jnp.float32,
    ).reshape(hit.shape)
    row_of = jnp.where(hit, ranks.astype(jnp.int32), -1)[:, :, None]
    placer = (
        (row_of == jnp.arange(capacity, dtype=jnp.int32)[:, None])
        .astype(jnp.bfloat16)
        .reshape(n_zh, n_near * capacity, tok_rows)
    )
    outgoing = lax.dot_general(
        placer, known_tokens, (((2,), (1,)), ((0,), (0,))), preferred_element_type=jnp.float32
    ).astype(jnp.bfloat16)
    outgoing = outgoing.reshape(n_zh, n_near, capacity, width_part).transpose(1, 0, 2, 3)
    outgoing, weights = lax.optimization_barrier((outgoing, weights))
    own_width = lax.all_to_all(outgoing, near, split_axis=0, concat_axis=0, tiled=True)
    own_width = own_width.transpose(1, 0, 2, 3)
    by_share = own_width.reshape(n_dp, share_rows, width_part)
    arrived = lax.all_to_all(by_share, "dp", split_axis=0, concat_axis=0, tiled=True)
    hidden, both_delta = experts(arrived, weights, hidden_grad[0])
    all_delta = lax.all_gather(both_delta, "dp", axis=0, tiled=True)
    def go_back(both_delta, weights, placer):
        slot_grad = slot_grads(both_delta, weights, n_dp)
        back = lax.all_to_all(slot_grad, "dp", split_axis=0, concat_axis=0, tiled=True)
        back = back.reshape(n_zh, n_near, capacity, width_part).transpose(1, 0, 2, 3)
        returned = lax.all_to_all(back, near, split_axis=0, concat_axis=0, tiled=True)
        returned = returned.transpose(1, 0, 2, 3).reshape(n_zh, n_near * capacity, width_part)
        token_sum = lax.dot_general(
            placer, returned, (((1,), (1,)), ((0,), (0,))), preferred_element_type=jnp.float32
        )
        sums = lax.all_to_all(
            token_sum.astype(jnp.bfloat16), "zh", split_axis=0, concat_axis=0, tiled=True
        )
        return jnp.sum(sums.astype(jnp.float32), axis=0).astype(jnp.bfloat16)

    token_grad = lax.cond(
        expert_ids[0, 0] >= 0, go_back, lambda *_: jnp.zeros_like(tokens), both_delta, weights, placer
    )

    rows = by_share.reshape(n_dp * share_rows, width_part).T
    gate_grad, up_grad = weight_grads(rows, all_delta)
    return hidden[None], gate_grad[None], up_grad[None], token_grad


def solution(mesh):
    n_expert, n_dp = mesh.devices.shape
    split = Mesh(mesh.devices.reshape(n_expert // (ZL * CORES), ZL, CORES, n_dp), ("zh", "zl", "c", "dp"))
    expert = ("zh", "zl", "c")
    placed = (
        P(expert, "dp"),
        P(expert, None),
        P(expert, "dp", None),
        P(expert, "dp", None),
        P(expert, "dp", None),
    )
    return jax.shard_map(
        on_device,
        mesh=split,
        in_specs=placed,
        out_specs=(
            P(expert, "dp", None),
            P(expert, "dp", None),
            P(expert, "dp", None),
            P(expert, "dp"),
        ),
        check_vma=False,
    )
```

```python
import jax
import jax.numpy as jnp
from jax import lax
from jax.experimental import pallas as pl
from jax.experimental.pallas import tpu as pltpu
from jax.sharding import Mesh, PartitionSpec as P

CORES = 2
ZL = 4


def expert_kernel(rows_ref, weights_ref, grad_ref, hidden_ref, delta_ref):
    n_dp = rows_ref.shape[0]
    hidden_units = grad_ref.shape[1]
    rows = jnp.concatenate([rows_ref[part] for part in range(n_dp)], axis=1)
    both = jnp.dot(rows, weights_ref[...], preferred_element_type=jnp.float32)
    gate, up = both[:, :hidden_units], both[:, hidden_units:]
    sigmoid_gate = jax.nn.sigmoid(gate)
    silu_gate = gate * sigmoid_gate
    hidden_ref[...] = (silu_gate * up).astype(jnp.bfloat16)
    grad = grad_ref[...].astype(jnp.float32)
    delta_ref[:, :hidden_units] = (
        grad * up * sigmoid_gate * (1.0 + gate * (1.0 - sigmoid_gate))
    ).astype(jnp.bfloat16)
    delta_ref[:, hidden_units:] = (grad * silu_gate).astype(jnp.bfloat16)


def experts(rows, weights, grad):
    share_rows, hidden_units = grad.shape
    return pl.pallas_call(
        expert_kernel,
        out_shape=(
            jax.ShapeDtypeStruct((share_rows, hidden_units), jnp.bfloat16),
            jax.ShapeDtypeStruct((share_rows, 2 * hidden_units), jnp.bfloat16),
        ),
        compiler_params=pltpu.CompilerParams(vmem_limit_bytes=32 * 1024 * 1024),
        cost_estimate=pl.CostEstimate(
            flops=2 * share_rows * weights.size,
            bytes_accessed=2 * weights.size,
            transcendentals=grad.size,
        ),
    )(rows, weights, grad)


def slot_grad_kernel(delta_ref, weights_ref, slot_grad_ref):
    n_dp, _, width_part = slot_grad_ref.shape
    delta = delta_ref[...]
    for part in range(n_dp):
        slot_grad_ref[part] = lax.dot_general(
            delta,
            weights_ref[part * width_part : (part + 1) * width_part],
            (((1,), (1,)), ((), ())),
            preferred_element_type=jnp.float32,
        ).astype(jnp.bfloat16)


def slot_grads(delta, weights, n_dp):
    share_rows = delta.shape[0]
    return pl.pallas_call(
        slot_grad_kernel,
        out_shape=jax.ShapeDtypeStruct(
            (n_dp, share_rows, weights.shape[0] // n_dp), jnp.bfloat16
        ),
        compiler_params=pltpu.CompilerParams(vmem_limit_bytes=32 * 1024 * 1024),
        cost_estimate=pl.CostEstimate(
            flops=2 * share_rows * weights.size,
            bytes_accessed=2 * weights.size,
            transcendentals=0,
        ),
    )(delta, weights)


def copies_kernel(gate_ref, up_ref, out_ref, rows, sems):
    hidden_units = gate_ref.shape[2]
    rows[:, :hidden_units] = gate_ref[0]
    rows[:, hidden_units:] = up_ref[0]
    copies = [
        pltpu.make_async_copy(rows, out_ref.at[part], sems.at[part])
        for part in range(out_ref.shape[0])
    ]
    for copy in copies:
        copy.start()
    for copy in copies:
        copy.wait()


def weight_copies(gate_w, up_w, n_dp):
    _, rows, hidden_units = gate_w.shape
    return pl.pallas_call(
        copies_kernel,
        out_shape=jax.ShapeDtypeStruct((n_dp, rows, 2 * hidden_units), gate_w.dtype),
        out_specs=pl.BlockSpec(memory_space=pl.ANY),
        scratch_shapes=[
            pltpu.VMEM((rows, 2 * hidden_units), gate_w.dtype),
            pltpu.SemaphoreType.DMA((n_dp,)),
        ],
    )(gate_w, up_w)


def on_device(tokens, expert_ids, gate_weight, up_weight, hidden_grad):
    n_zh = lax.axis_size("zh")
    n_dp = lax.axis_size("dp")
    near = ("zl", "c")
    tok_rows, width_part = tokens.shape
    top_k = expert_ids.shape[1]
    share_rows = hidden_grad.shape[1]
    hidden_units = gate_weight.shape[2]
    capacity = share_rows * n_dp // (n_zh * ZL * CORES)

    weights = weight_copies(gate_weight, up_weight, n_dp)
    weights = lax.all_to_all(weights, "dp", split_axis=0, concat_axis=0, tiled=True)
    weights = weights.reshape(-1, 2 * hidden_units)

    ids_rows = expert_ids.T.astype(jnp.bfloat16)
    sent = jnp.concatenate([tokens, ids_rows], axis=0)
    known = lax.all_gather(sent, "zh", axis=0, tiled=False)
    known_tokens = known[:, :tok_rows]
    known_ids = known[:, tok_rows:].astype(jnp.float32)

    n_near = ZL * CORES
    expert_of = lax.axis_index("zh") * n_near + jnp.arange(n_near, dtype=jnp.int32)
    expert_of = expert_of.astype(jnp.float32)[None, :, None]
    hit = jnp.zeros((n_zh, n_near, tok_rows), jnp.bool_)
    for choice_k in range(top_k):
        hit = hit | (known_ids[:, choice_k][:, None] == expert_of)
    earlier = jnp.arange(tok_rows)[:, None] < jnp.arange(tok_rows)[None, :]
    ranks = jnp.dot(
        hit.reshape(-1, tok_rows).astype(jnp.bfloat16),
        earlier.astype(jnp.bfloat16),
        preferred_element_type=jnp.float32,
    ).reshape(hit.shape)
    row_of = jnp.where(hit, ranks.astype(jnp.int32), -1)[:, :, None]
    placer = (
        (row_of == jnp.arange(capacity, dtype=jnp.int32)[:, None])
        .astype(jnp.bfloat16)
        .reshape(n_zh, n_near * capacity, tok_rows)
    )
    outgoing = lax.dot_general(
        placer, known_tokens, (((2,), (1,)), ((0,), (0,))), preferred_element_type=jnp.float32
    ).astype(jnp.bfloat16)
    outgoing = outgoing.reshape(n_zh, n_near, capacity, width_part).transpose(1, 0, 2, 3)
    outgoing, weights = lax.optimization_barrier((outgoing, weights))
    own_width = lax.all_to_all(outgoing, near, split_axis=0, concat_axis=0, tiled=True)
    own_width = own_width.transpose(1, 0, 2, 3)
    by_share = own_width.reshape(n_dp, share_rows, width_part)
    arrived = lax.all_to_all(by_share, "dp", split_axis=0, concat_axis=0, tiled=True)
    hidden, both_delta = experts(arrived, weights, hidden_grad[0])
    all_delta = lax.all_gather(both_delta, "dp", axis=0, tiled=True)
    def go_back(both_delta, weights, placer):
        slot_grad = slot_grads(both_delta, weights, n_dp)
        back = lax.all_to_all(slot_grad, "dp", split_axis=0, concat_axis=0, tiled=True)
        back = back.reshape(n_zh, n_near, capacity, width_part).transpose(1, 0, 2, 3)
        returned = lax.all_to_all(back, near, split_axis=0, concat_axis=0, tiled=True)
        returned = returned.transpose(1, 0, 2, 3).reshape(n_zh, n_near * capacity, width_part)
        token_sum = lax.dot_general(
            placer, returned, (((1,), (1,)), ((0,), (0,))), preferred_element_type=jnp.float32
        )
        sums = lax.all_to_all(
            token_sum.astype(jnp.bfloat16), "zh", split_axis=0, concat_axis=0, tiled=True
        )
        return jnp.sum(sums.astype(jnp.float32), axis=0).astype(jnp.bfloat16)

    token_grad = lax.cond(
        expert_ids[0, 0] >= 0, go_back, lambda *_: jnp.zeros_like(tokens), both_delta, weights, placer
    )

    both_grad = lax.dot_general(
        own_width.reshape(n_dp * share_rows, width_part),
        all_delta,
        (((0,), (0,)), ((), ())),
        preferred_element_type=jnp.float32,
    )
    return (
        hidden[None],
        both_grad[None, :, :hidden_units],
        both_grad[None, :, hidden_units:],
        token_grad,
    )


def solution(mesh):
    n_expert, n_dp = mesh.devices.shape
    split = Mesh(mesh.devices.reshape(n_expert // (ZL * CORES), ZL, CORES, n_dp), ("zh", "zl", "c", "dp"))
    expert = ("zh", "zl", "c")
    placed = (
        P(expert, "dp"),
        P(expert, None),
        P(expert, "dp", None),
        P(expert, "dp", None),
        P(expert, "dp", None),
    )
    return jax.shard_map(
        on_device,
        mesh=split,
        in_specs=placed,
        out_specs=(
            P(expert, "dp", None),
            P(expert, "dp", None),
            P(expert, "dp", None),
            P(expert, "dp"),
        ),
        check_vma=False,
    )
```
